32 devices in a mesh: district: 2 (over x), tiles: 16 (over z, y, core).
Axes of the slice: x: 2, y: 2, z: 4, core: 2. Of those that a mesh axis runs over, the one named last changes fastest.
Arguments:
- sky: bfloat16 [336, 2306], P('district'), parts along dimension 0, may hold values from -6 to 6
- coeffs: bfloat16 [2306, 32768], P(None, ('district', 'tiles')), parts along dimension 1, may hold values from -0.125 to 0.125
- albedo: float32 [32768], P(('district', 'tiles')), parts along dimension 0, may hold values from 0.1 to 0.9
- view_blocks: bfloat16 [2048, 128, 128], P(('district', 'tiles')), parts along dimension 0, may hold values from -0.1875 to 0.1875
- block_rows: int32 [2048], P(('district', 'tiles')), parts along dimension 0, may hold values from 0 to 127, as said below
- block_cols: int32 [2048], P(('district', 'tiles')), parts along dimension 0, may hold values from 0 to 127, as said below
- counts: int32 [32], P(('district', 'tiles')), parts along dimension 0, may hold values from 8 to 64, as said below
Outputs:
- irradiance: float32 [168, 32768], P(None, ('district', 'tiles')), parts along dimension 1
The draws below stay inside these ranges and needn't reach their ends.
There are 2 independent parts, one for each index of `district`. The reference program is written for one: setup_inputs(seed, part) draws one part's arguments, and reference() takes and returns one part's arrays. A program takes and returns all parts, laid end to end along the dimension named above; each array names one. Nothing has to cross between parts.
Inputs may be any that keep to these rules, and one draw needn't show every extreme that they name: `block_rows`: slots of group g (slots g * 64 to (g + 1) * 64 - 1) name receiving blocks of group g's own tiles, that is g * 8 to (g + 1) * 8 - 1. `block_cols`: the slots of one group name at most 2 distinct sending blocks among the tiles of any one group, and exactly 2 among those of some group. Slots of group g at positions counts[g] and beyond are unused; some group has all 64 slots live.
All inputs are finite; a program needn't handle non-finite values.
Results may differ from the reference program's by a relative error of at most 0.0011.
Values may be sent and summed in bfloat16 or wider, within the bound.
No kernel may reach another device: no remote copies, remote signals or barrier semaphores. Data moves between devices by JAX's collectives and lax.ppermute only.
A program may use at most 128 MiB of HBM per device.

```python
import jax
import jax.numpy as jnp
from jax import lax

PATCH = 2306
HOURS = 168
BLK = 128
TILE_DEV = 1024
NB_DEV = 64
CAP = 2
TILES = 16384
SLOTS = 1024
N_TILES = 16


def pattern(key):
    base_key = jax.random.fold_in(key, 7)
    key_rows, key_near, key_far, key_pick, key_offs, key_slot, key_lead = jax.random.split(base_key, 7)
    per_group = TILE_DEV // BLK
    groups = N_TILES
    device = jnp.arange(groups, dtype=jnp.int32)[:, None] * jnp.ones((1, NB_DEV), jnp.int32)
    rows_all = device * per_group + jax.random.randint(key_rows, (groups, NB_DEV), 0, per_group)
    nearby = jax.random.randint(key_near, (groups, NB_DEV), -2, 3)
    distant = jax.random.randint(key_far, (groups, NB_DEV), 0, groups)
    chooser = jax.random.randint(key_pick, (groups, NB_DEV), 0, 2)
    source = jnp.where(chooser == 0, (device + nearby) % groups, distant)
    offsets = jax.random.randint(key_offs, (groups, groups), 0, per_group)
    slot_pick = jax.random.randint(key_slot, (groups, NB_DEV), 0, CAP)
    within = (jnp.take_along_axis(offsets, source, axis=1) + slot_pick) % per_group
    leader = jax.random.randint(key_lead, (groups, 1), 0, groups)
    slot_index = jnp.arange(NB_DEV, dtype=jnp.int32)[None, :]
    leading = slot_index < CAP
    lead_within = (jnp.take_along_axis(offsets, leader, axis=1) + slot_index) % per_group
    source = jnp.where(leading, leader, source)
    within = jnp.where(leading, lead_within, within)
    cols_all = source * per_group + within
    return (rows_all.reshape(-1), cols_all.reshape(-1))


def draw_block_rows(key, part):
    return pattern(key)[0]


def draw_block_cols(key, part):
    return pattern(key)[1]


def draw_counts(key, part):
    key_exp, key_full = jax.random.split(jax.random.fold_in(key, 11))
    powers = jax.random.randint(key_exp, (N_TILES,), 0, 4)
    values = jnp.right_shift(jnp.full((N_TILES,), NB_DEV, jnp.int32), powers)
    fullest = jax.random.randint(key_full, (), 0, N_TILES)
    return jnp.where(jnp.arange(N_TILES, dtype=jnp.int32) == fullest, NB_DEV, values).astype(jnp.int32)


def block_scale(key, shape, cuts, smallest, top_value):
    gain = 1.0
    for axis_at, parts in cuts:
        steps = jax.random.uniform(jax.random.fold_in(jax.random.fold_in(key, 6), axis_at), (parts,), jnp.float32, smallest / len(cuts), top_value / len(cuts))
        gain = gain * jnp.repeat(jnp.exp(steps), shape[axis_at] // parts).reshape((-1,) + (1,) * (len(shape) - 1 - axis_at))
    return gain


def normal_values(rng, dims, spread, limit, cuts=(), held_as=jnp.bfloat16):
    loudness = block_scale(rng, dims, cuts, -0.22, 0.18) if cuts else 1.0
    values = jax.random.normal(rng, dims, jnp.float32) * spread * loudness
    return jnp.minimum(jnp.maximum(values, -limit), limit).astype(held_as)


def setup_inputs(seed: int = 0, part: int = 0) -> dict:
    splits = jax.random.split(jax.random.key(seed), 8)
    own_keys = jax.random.split(jax.random.fold_in(splits[7], part), 8)
    sky = normal_values(own_keys[0], (HOURS, PATCH), 1.0, 6.0)
    coeffs = normal_values(own_keys[1], (PATCH, TILES), PATCH ** -0.5, 0.125, ((1, 16),))
    albedo = jnp.clip(0.1 + 0.79999997 * jax.random.uniform(own_keys[2], (TILES,), jnp.float32) ** block_scale(own_keys[2], (TILES,), ((0, 16),), -0.2, 0.2), 0.1, 0.9)
    view_blocks = normal_values(own_keys[3], (SLOTS, BLK, BLK), (BLK * NB_DEV * BLK // TILE_DEV) ** -0.5, 0.1875, ((0, 16),))
    block_rows = draw_block_rows(jax.random.fold_in(jax.random.fold_in(splits[7], part), 71), part)
    block_cols = draw_block_cols(jax.random.fold_in(jax.random.fold_in(splits[7], part), 71), part)
    counts = draw_counts(jax.random.fold_in(jax.random.fold_in(splits[7], part), 71), part)
    return {"sky": sky, "coeffs": coeffs, "albedo": albedo, "view_blocks": view_blocks, "block_rows": block_rows, "block_cols": block_cols, "counts": counts}


def reference(sky, coeffs, albedo, view_blocks, block_rows, block_cols, counts):
    direct = jnp.dot(sky, coeffs, preferred_element_type=jnp.float32)
    emitted = (albedo[None, :] * direct).astype(jnp.bfloat16)
    source_pool = emitted.reshape(HOURS, TILES // BLK, BLK)
    per_group = TILE_DEV // BLK

    def one_group(packed):
        values, rows_here, cols_here, count_here, group = packed
        sources = jnp.take(source_pool, cols_here, axis=1).astype(jnp.float32)
        contrib = jnp.einsum("bij,hbj->bhi", values.astype(jnp.float32), sources, precision=lax.Precision.HIGHEST)
        live_slots = jnp.arange(NB_DEV, dtype=jnp.int32) < count_here
        local_rows = rows_here - group * per_group
        onehot = (local_rows[None, :] == jnp.arange(per_group, dtype=jnp.int32)[:, None]) & live_slots[None, :]
        return jnp.einsum("rb,bhi->hri", onehot.astype(jnp.float32), contrib, precision=lax.Precision.HIGHEST)

    grouped = lax.map(one_group, (view_blocks.reshape(N_TILES, NB_DEV, BLK, BLK), block_rows.reshape(N_TILES, NB_DEV), block_cols.reshape(N_TILES, NB_DEV), counts, jnp.arange(N_TILES, dtype=jnp.int32)))
    reflected = jnp.transpose(grouped, (1, 0, 2, 3)).reshape(HOURS, TILES)
    return direct + reflected
```

```python
import functools

import jax
import jax.numpy as jnp
from jax import lax
from jax.experimental import pallas as pl
from jax.experimental.pallas import tpu as pltpu
from jax.sharding import PartitionSpec as P

NEAR = 8
AT_ONCE = 8
SMEM = pl.BlockSpec(memory_space=pltpu.SMEM)
VMEM = pl.BlockSpec(memory_space=pltpu.VMEM)
ANY = pl.BlockSpec(memory_space=pl.ANY)


def direct_kernel(sky_ref, coeffs_ref, albedo_ref, direct_ref, emitted_ref):
    direct = jnp.dot(sky_ref[...], coeffs_ref[...], preferred_element_type=jnp.float32)
    direct_ref[...] = direct
    emitted = (albedo_ref[...] * direct).astype(jnp.bfloat16)
    block = emitted_ref.shape[2]
    for at in range(emitted_ref.shape[0]):
        emitted_ref[at] = emitted[:, at * block : (at + 1) * block]


def direct_and_emitted(sky, coeffs, albedo, block, width):
    hours, patches = sky.shape
    tiles = coeffs.shape[1]
    return pl.pallas_call(
        direct_kernel,
        grid=(tiles // width,),
        in_specs=[
            pl.BlockSpec((hours, patches), lambda i: (0, 0)),
            pl.BlockSpec((patches, width), lambda i: (0, i)),
            pl.BlockSpec((1, width), lambda i: (0, i)),
        ],
        out_specs=[
            pl.BlockSpec((hours, width), lambda i: (0, i)),
            pl.BlockSpec((width // block, hours, block), lambda i: (i, 0, 0)),
        ],
        out_shape=[
            jax.ShapeDtypeStruct((hours, tiles), jnp.float32),
            jax.ShapeDtypeStruct((tiles // block, hours, block), jnp.bfloat16),
        ],
        compiler_params=pltpu.CompilerParams(vmem_limit_bytes=56 * 2**20),
        name="direct",
    )(sky, coeffs, albedo)


def pack_kernel(wanted, me_ref, table_ref, *refs):
    count = len(wanted)
    held, outs, sems = refs[: -count - 1], refs[-count - 1 : -1], refs[-1]
    copies = []
    for out, sends in zip(outs, wanted):
        for at, (which, bits, row, end) in enumerate(sends):
            block = table_ref[row, 2 * (me_ref[0] ^ bits) + end]
            copies.append(pltpu.make_async_copy(held[which].at[block], out.at[at], sems.at[len(copies)]))
    for copy in copies:
        copy.start()
    for copy in copies:
        copy.wait()


def pack(me, table, held, wanted):
    return pl.pallas_call(
        functools.partial(pack_kernel, wanted),
        in_specs=[SMEM, SMEM] + [VMEM] * len(held),
        out_specs=[ANY] * len(wanted),
        out_shape=[jax.ShapeDtypeStruct((len(sends),) + held[0].shape[1:], held[0].dtype) for sends in wanted],
        scratch_shapes=[pltpu.SemaphoreType.DMA((sum(map(len, wanted)),))],
        compiler_params=pltpu.CompilerParams(vmem_limit_bytes=24 * 2**20),
        name="pack",
    )(me, table, *held)


def plan_kernel(blocks, rooms, me_ref, count_ref, rows_ref, cols_ref, hi_ref, phase_ref, base_ref, order_ref, size_ref):
    phases, places = order_ref.shape
    for at in range(phases):
        size_ref[at] = 0

    def clear(i, carry):
        for at in range(phases):
            order_ref[at, i] = rooms[at] * 4096
        return carry

    lax.fori_loop(0, places, clear, 0)

    def step(slot, carry):
        col = cols_ref[slot]
        group = col // blocks
        kind = group ^ me_ref[0]
        inside = col - group * blocks
        local = (kind & (NEAR - 2)) == 0
        end = (inside == hi_ref[group]).astype(jnp.int32)
        source = base_ref[kind] + jnp.where(local, inside, end)
        row = rows_ref[slot] - me_ref[0] * blocks
        phase = phase_ref[kind]
        at = size_ref[phase]
        order_ref[phase, at] = slot + row * 256 + source * 4096
        size_ref[phase] = at + 1
        return carry

    lax.fori_loop(0, count_ref[0], step, 0)


def plan(me, counts, rows, cols, hi, phase, base, blocks, rooms):
    return pl.pallas_call(
        functools.partial(plan_kernel, blocks, rooms),
        in_specs=[SMEM] * 7,
        out_specs=[SMEM, SMEM],
        out_shape=[
            jax.ShapeDtypeStruct((len(rooms), rows.shape[0] + AT_ONCE), jnp.int32),
            jax.ShapeDtypeStruct((len(rooms),), jnp.int32),
        ],
        name="plan",
    )(me, counts, rows, cols, hi, phase, base)


def reflect_kernel(phase, order_ref, size_ref, total_ref, views_ref, *refs):
    sources, out_ref, pool, sems = refs[:-3], refs[-3], refs[-2], refs[-1]
    copies = []
    room = 0
    for number, source in enumerate(sources):
        length = source.shape[0]
        copies.append(pltpu.make_async_copy(source, pool.at[pl.ds(room, length)], sems.at[number]))
        room += length
    for copy in copies:
        copy.start()
    out_ref[...] = total_ref[...]
    pool[room] = jnp.zeros(pool.shape[1:], pool.dtype)
    for copy in copies:
        copy.wait()
    block = views_ref.shape[1]

    def step(i, carry):
        entries = [order_ref[phase, i * AT_ONCE + k] for k in range(AT_ONCE)]
        parts = [
            lax.dot_general(
                pool[entry // 4096],
                views_ref[entry & 255],
                (((1,), (1,)), ((), ())),
                preferred_element_type=jnp.float32,
            )
            for entry in entries
        ]
        for entry, part in zip(entries, parts):
            columns = pl.ds(pl.multiple_of(((entry // 256) & 15) * block, block), block)
            out_ref[:, columns] += part
        return carry

    lax.fori_loop(0, (size_ref[phase] + AT_ONCE - 1) // AT_ONCE, step, 0)


def reflect(phase, order, size, total, views, sources):
    room = sum(source.shape[0] for source in sources)
    return pl.pallas_call(
        functools.partial(reflect_kernel, phase),
        in_specs=[SMEM, SMEM, VMEM, VMEM] + [ANY] * len(sources),
        out_specs=VMEM,
        out_shape=jax.ShapeDtypeStruct(total.shape, total.dtype),
        scratch_shapes=[
            pltpu.VMEM((room + 1,) + sources[0].shape[1:], sources[0].dtype),
            pltpu.SemaphoreType.DMA((len(sources),)),
        ],
        compiler_params=pltpu.CompilerParams(vmem_limit_bytes=24 * 2**20),
        name="reflect",
    )(order, size, total, views, *sources)


def per_device(sky, coeffs, albedo, view_blocks, block_rows, block_cols, counts):
    peers = lax.axis_size("tiles")
    me = lax.axis_index("tiles").astype(jnp.int32).reshape(1)
    slots, block = view_blocks.shape[:2]
    blocks = coeffs.shape[1] // block
    rest = peers // NEAR - 1
    far = [NEAR * k for k in range(1, rest + 1)]
    steps = range(2, NEAR, 2)

    def swap(x, bits):
        return lax.ppermute(x, "tiles", [(i, i ^ bits) for i in range(peers)])

    direct, emitted = direct_and_emitted(sky, coeffs, albedo.reshape(1, -1), block, 2 * block)
    block_cols, counts, emitted = lax.optimization_barrier((block_cols, counts, emitted))

    far_held = [swap(emitted, bits) for bits in far]
    near_held = [emitted, swap(emitted, 1)]

    live = jnp.arange(slots, dtype=jnp.int32) < counts[0]
    reads = (block_cols // blocks == jnp.arange(peers, dtype=jnp.int32)[:, None]) & live
    inside = block_cols % blocks
    lo = jnp.min(jnp.where(reads, inside, blocks - 1), axis=1)
    hi = jnp.max(jnp.where(reads, inside, 0), axis=1)
    table = jnp.stack([lo, hi], axis=1).reshape(1, 2 * peers)
    step = 2
    while step < NEAR:
        table = jnp.concatenate([table, swap(table, step)])
        step *= 2

    phase_of, base_of = [], []
    for kind in range(peers):
        core, row, h = kind % 2, kind % NEAR // 2, kind // NEAR - 1
        if h < 0:
            phase_of.append(0)
            base_of.append(blocks * core if row == 0 else 2 * blocks + 4 * (row - 1) + 2 * core)
        elif row == 0:
            phase_of.append(1)
            base_of.append(blocks * (2 * h + core))
        elif row == 1:
            phase_of.append(1)
            base_of.append(2 * blocks * rest + 4 * h + 2 * core)
        else:
            phase_of.append(2)
            base_of.append(4 * rest * (row - 2) + 4 * h + 2 * core)
    rooms = [2 * blocks + 4 * len(steps), (2 * blocks + 4) * rest, 4 * rest * (len(steps) - 1)]
    own = pack(me, table, near_held, [[(c, c, d // 2, end) for c in range(2) for end in range(2)] for d in steps])
    early = [swap(x, d) for x, d in zip(own, steps)]
    block_rows, _ = lax.optimization_barrier((block_rows, own[0]))
    order, size = plan(
        me,
        counts,
        block_rows,
        block_cols,
        hi,
        jnp.array(phase_of, jnp.int32),
        jnp.array(base_of, jnp.int32),
        blocks,
        rooms,
    )

    order, size, *far_held = lax.optimization_barrier((order, size, *far_held))

    held = [x for shard in far_held for x in (shard, swap(shard, 1))]
    others = pack(
        me,
        table,
        held,
        [
            [(2 * h + c, far[h] ^ c, d // 2, end) for h in range(rest) for c in range(2) for end in range(2)]
            for d in steps
        ],
    )
    late = {d: swap(x, d) for x, d in reversed(list(zip(others, steps)))}
    direct, _ = lax.optimization_barrier((direct, others[0]))
    total = reflect(0, order, size, direct, view_blocks, near_held + early)
    total = reflect(1, order, size, total, view_blocks, held + [late[2]])
    return reflect(2, order, size, total, view_blocks, [late[d] for d in steps[1:]])


def solution(mesh):
    in_specs = (
        P("district", None),
        P(None, ("district", "tiles")),
        P(("district", "tiles")),
        P(("district", "tiles"), None, None),
        P(("district", "tiles")),
        P(("district", "tiles")),
        P(("district", "tiles")),
    )
    out_specs = P(None, ("district", "tiles"))
    return jax.shard_map(
        per_device, mesh=mesh, in_specs=in_specs, out_specs=out_specs, check_vma=False
    )
```

```python
import functools

import jax
import jax.numpy as jnp
from jax import lax
from jax.experimental import pallas as pl
from jax.experimental.pallas import tpu as pltpu
from jax.sharding import PartitionSpec as P

NEAR = 8
AT_ONCE = 8
SMEM = pl.BlockSpec(memory_space=pltpu.SMEM)
VMEM = pl.BlockSpec(memory_space=pltpu.VMEM)
ANY = pl.BlockSpec(memory_space=pl.ANY)
HBM = pl.BlockSpec(memory_space=pltpu.HBM)


def direct_kernel(width, sky_ref, coeffs_ref, albedo_ref, direct_ref, emitted_ref, sky, coeffs, direct, sems):
    blocks, _, block = emitted_ref.shape
    parts = coeffs.shape[0]
    whole_sky = pltpu.make_async_copy(sky_ref, sky, sems.at[2 * parts])
    copies = [
        pltpu.make_async_copy(coeffs_ref.at[:, pl.ds(at * width, width)], coeffs.at[at], sems.at[at])
        for at in range(parts)
    ]
    results = [
        pltpu.make_async_copy(direct.at[at], direct_ref.at[:, pl.ds(at * width, width)], sems.at[parts + at])
        for at in range(parts)
    ]
    copies[0].start()
    whole_sky.start()
    for copy in copies[1:]:
        copy.start()
    whole_sky.wait()
    for at in range(parts):
        copies[at].wait()
        part = jnp.dot(sky[...], coeffs[at], preferred_element_type=jnp.float32)
        direct[at] = part
        results[at].start()
        emitted = (albedo_ref[:, at * width : (at + 1) * width] * part).astype(jnp.bfloat16)
        for k in range(width // block):
            emitted_ref[at * (width // block) + k] = emitted[:, k * block : (k + 1) * block]
    for result in results:
        result.wait()


def direct_and_emitted(sky, coeffs, albedo, block, width):
    hours, patches = sky.shape
    tiles = coeffs.shape[1]
    parts = tiles // width
    return pl.pallas_call(
        functools.partial(direct_kernel, width),
        in_specs=[HBM, HBM, VMEM],
        out_specs=[HBM, VMEM],
        out_shape=[
            jax.ShapeDtypeStruct((hours, tiles), jnp.float32),
            pltpu.VMEM((tiles // block, hours, block), jnp.bfloat16),
        ],
        scratch_shapes=[
            pltpu.VMEM(sky.shape, sky.dtype),
            pltpu.VMEM((parts, patches, width), coeffs.dtype),
            pltpu.VMEM((parts, hours, width), jnp.float32),
            pltpu.SemaphoreType.DMA((2 * parts + 1,)),
        ],
        compiler_params=pltpu.CompilerParams(vmem_limit_bytes=60 * 2**20),
        name="direct",
    )(sky, coeffs, albedo)


def reads_kernel(blocks, groups, cols_ref, reads_ref):
    slots, width = cols_ref.shape[1], reads_ref.shape[1]
    group = lax.broadcasted_iota(jnp.int32, (groups, slots), 0)
    inside = jnp.broadcast_to(cols_ref[...], (groups, slots)) - group * blocks
    read = (inside >= 0) & (inside < blocks)
    lo = jnp.min(jnp.where(read, inside, blocks - 1), axis=1, keepdims=True)
    hi = jnp.max(jnp.where(read, inside, 0), axis=1, keepdims=True)
    group = lax.broadcasted_iota(jnp.int32, (groups, width), 0)
    lane = lax.broadcasted_iota(jnp.int32, (groups, width), 1)
    row = jnp.where(lane == group, lo, 0) + jnp.where(lane == group + groups, hi, 0)
    live = jnp.sum((cols_ref[...] >= 0).astype(jnp.int32), axis=1, keepdims=True)
    reads_ref[...] = jnp.sum(row, axis=0, keepdims=True) + jnp.where(lane[0:1] == 2 * groups, live, 0)


def blocks_read(cols, blocks, groups):
    width = -(-(2 * groups + 1) // 128) * 128
    return pl.pallas_call(
        functools.partial(reads_kernel, blocks, groups),
        in_specs=[VMEM],
        out_specs=VMEM,
        out_shape=jax.ShapeDtypeStruct((1, width), jnp.int32),
        compiler_params=pltpu.CompilerParams(vmem_limit_bytes=2**20),
        name="reads",
    )(cols.reshape(1, -1))


def pack_kernel(wanted, groups, me_ref, table_ref, *refs):
    held, outs = refs[: -len(wanted)], refs[-len(wanted) :]
    for out, (peer, sends) in zip(outs, wanted):
        for at, (which, bits, end) in enumerate(sends):
            out[at] = held[which][table_ref[peer, (me_ref[0] ^ bits) + groups * end]]


def pack(me, table, groups, held, wanted):
    return pl.pallas_call(
        functools.partial(pack_kernel, wanted, groups),
        in_specs=[SMEM, SMEM] + [VMEM] * len(held),
        out_specs=[VMEM] * len(wanted),
        out_shape=[pltpu.VMEM((len(sends),) + held[0].shape[1:], held[0].dtype) for _, sends in wanted],
        compiler_params=pltpu.CompilerParams(vmem_limit_bytes=24 * 2**20),
        name="pack",
    )(me, table, *held)


def plan_kernel(blocks, rooms, groups, me_ref, rows_ref, cols_ref, reads_ref, phase_ref, base_ref, local_ref, after_ref, order_ref):
    del after_ref
    phases, places = order_ref.shape

    def clear(i, carry):
        for at in range(phases):
            order_ref[at, i] = rooms[at] * 4096
        return carry

    lax.fori_loop(1, places, clear, 0)
    for at in range(phases):
        order_ref[at, 0] = 0

    def step(slot, carry):
        col = cols_ref[slot]
        group = col // blocks
        kind = group ^ me_ref[0]
        inside = col - group * blocks
        local = local_ref[kind] == 1
        end = (inside == reads_ref[0, groups + group]).astype(jnp.int32)
        source = base_ref[kind] + jnp.where(local, inside, end)
        row = rows_ref[slot] - me_ref[0] * blocks
        phase = phase_ref[kind]
        at = order_ref[phase, 0] + 1
        order_ref[phase, at] = slot + row * 256 + source * 4096
        order_ref[phase, 0] = at
        return carry

    lax.fori_loop(0, reads_ref[0, 2 * groups], step, 0)


def plan(me, rows, cols, reads, phase, base, local, after, blocks, rooms):
    return pl.pallas_call(
        functools.partial(plan_kernel, blocks, rooms, phase.shape[0]),
        in_specs=[SMEM] * 7 + [ANY],
        out_specs=SMEM,
        out_shape=jax.ShapeDtypeStruct((len(rooms), 1 + rows.shape[0] + AT_ONCE), jnp.int32),
        compiler_params=pltpu.CompilerParams(vmem_limit_bytes=2**20),
        name="plan",
    )(me, rows, cols, reads, phase, base, local, after)


def reflect_kernel(phase, order_ref, total_ref, views_ref, *refs):
    sources, (out_ref, pool, order, sems) = refs[:-4], refs[-4:]
    copies = [
        pltpu.make_async_copy(total_ref, out_ref, sems.at[len(sources)]),
        pltpu.make_async_copy(order_ref, order, sems.at[len(sources) + 1]),
    ]
    room = 0
    for number, source in enumerate(sources):
        length = source.shape[0]
        copies.append(pltpu.make_async_copy(source, pool.at[pl.ds(room, length)], sems.at[number]))
        room += length
    for copy in copies:
        copy.start()
    pool[room] = jnp.zeros(pool.shape[1:], pool.dtype)
    for copy in copies:
        copy.wait()
    block = views_ref.shape[1]

    def step(i, carry):
        entries = [order[phase, 1 + i * AT_ONCE + k] for k in range(AT_ONCE)]
        parts = [
            lax.dot_general(
                pool[entry // 4096],
                views_ref[entry & 255],
                (((1,), (1,)), ((), ())),
                preferred_element_type=jnp.float32,
            )
            for entry in entries
        ]
        for entry, part in zip(entries, parts):
            columns = pl.ds(pl.multiple_of(((entry // 256) & 15) * block, block), block)
            out_ref[:, columns] += part
        return carry

    lax.fori_loop(0, (order[phase, 0] + AT_ONCE - 1) // AT_ONCE, step, 0)


def reflect(phase, order, total, views, sources):
    room = sum(source.shape[0] for source in sources)
    return pl.pallas_call(
        functools.partial(reflect_kernel, phase),
        in_specs=[HBM, HBM if phase == 0 else ANY, VMEM] + [ANY] * len(sources),
        out_specs=VMEM,
        out_shape=jax.ShapeDtypeStruct(total.shape, total.dtype),
        scratch_shapes=[
            pltpu.VMEM((room + 1,) + sources[0].shape[1:], sources[0].dtype),
            pltpu.SMEM(order.shape, order.dtype),
            pltpu.SemaphoreType.DMA((len(sources) + 2,)),
        ],
        compiler_params=pltpu.CompilerParams(vmem_limit_bytes=24 * 2**20),
        name="reflect",
    )(order, total, views, *sources)


def per_device(sky, coeffs, albedo, view_blocks, block_rows, block_cols, counts):
    peers = lax.axis_size("tiles")
    me = lax.axis_index("tiles").astype(jnp.int32).reshape(1)
    block = view_blocks.shape[1]
    blocks = coeffs.shape[1] // block
    rest = peers // NEAR - 1
    far = [NEAR * k for k in range(1, rest + 1)]
    core, beside, below = 1, 2, 4

    def swap(x, bits):
        return lax.ppermute(x, "tiles", [(i, i ^ bits) for i in range(peers)])

    direct, emitted = direct_and_emitted(sky, coeffs, albedo.reshape(1, -1), block, 4 * block)
    counts, view_blocks, emitted = lax.optimization_barrier((counts, view_blocks, emitted))

    far_held = [swap(emitted, bits) for bits in far]
    below_held = swap(emitted, below)
    beside_held = swap(emitted, beside)

    live = jnp.arange(block_cols.shape[0], dtype=jnp.int32) < counts[0]
    reads = blocks_read(jnp.where(live, block_cols, -1), blocks, peers)
    core_reads = swap(reads, core)
    table = jnp.concatenate([reads, swap(reads, beside)])
    below_table = swap(table, below)

    (own,) = pack(
        me, core_reads, peers, [emitted, beside_held], [(0, [(h, h * beside, end) for h in range(2) for end in range(2)])]
    )
    own = swap(own, core)

    place = {
        0: (0, 0),
        beside: (0, blocks),
        core: (0, 2 * blocks),
        beside + core: (0, 2 * blocks + 2),
        below: (1, 2 * blocks * rest),
        below + core: (1, 2 * blocks * rest + blocks),
        below + beside + core: (1, 2 * blocks * (rest + 1) + 4 * rest),
        below + beside: (2, 4 * rest),
    }
    local = {0, beside, below, below + core}
    for h, bits in enumerate(far):
        for c in range(2):
            local.add(bits + c)
            place[bits + c] = (1, blocks * (2 * h + c))
            place[bits + beside + c] = (1, 2 * blocks * (rest + 1) + 4 * h + 2 * c)
            place[bits + below + c] = (2, 4 * h + 2 * c)
            place[bits + below + beside + c] = (2, 4 * rest + 2 + 4 * h + 2 * c)
    rooms = [2 * blocks + 4, 2 * blocks * (rest + 1) + 4 * rest + 2, 8 * rest + 2]
    order = plan(
        me,
        block_rows,
        block_cols,
        reads,
        jnp.array([place[kind][0] for kind in range(peers)], jnp.int32),
        jnp.array([place[kind][1] for kind in range(peers)], jnp.int32),
        jnp.array([int(kind in local) for kind in range(peers)], jnp.int32),
        own,
        blocks,
        rooms,
    )
    order, below_table, below_held, far_held = lax.optimization_barrier((order, below_table, below_held, far_held))
    table = jnp.concatenate([table, below_table])
    held = [x for shard in far_held for x in (shard, swap(shard, core))]
    below_pair = [below_held, swap(below_held, core)]

    wanted = [(2 * h + c, far[h] + c, end) for h in range(rest) for c in range(2) for end in range(2)]
    from_beside = [(2 * rest, below + core, end) for end in range(2)]
    from_below = [(2 * rest + 1, beside, end) for end in range(2)]
    sends = [(1, wanted + from_beside), (2, wanted + from_below), (3, wanted)]
    others = pack(me, table, peers, held + [below_pair[1], beside_held], sends)
    late = [swap(x, bits) for x, bits in zip(others, (beside, below, below + beside))]

    direct, _ = lax.optimization_barrier((direct, others[0]))
    total = reflect(0, order, direct, view_blocks, [emitted, beside_held, own])
    total = reflect(1, order, total, view_blocks, held + below_pair + late[:1])
    return reflect(2, order, total, view_blocks, late[1:])


def solution(mesh):
    in_specs = (
        P("district", None),
        P(None, ("district", "tiles")),
        P(("district", "tiles")),
        P(("district", "tiles"), None, None),
        P(("district", "tiles")),
        P(("district", "tiles")),
        P(("district", "tiles")),
    )
    out_specs = P(None, ("district", "tiles"))
    return jax.shard_map(
        per_device, mesh=mesh, in_specs=in_specs, out_specs=out_specs, check_vma=False
    )
```

```python
import functools

import jax
import jax.numpy as jnp
from jax import lax
from jax.experimental import pallas as pl
from jax.experimental.pallas import tpu as pltpu
from jax.sharding import PartitionSpec as P

NEAR = 8
AT_ONCE = 8
SMEM = pl.BlockSpec(memory_space=pltpu.SMEM)
VMEM = pl.BlockSpec(memory_space=pltpu.VMEM)
ANY = pl.BlockSpec(memory_space=pl.ANY)
HBM = pl.BlockSpec(memory_space=pltpu.HBM)


def product_kernel(width, after_ref, sky_ref, coeffs_ref, albedo_ref, out_ref, last_ref, sky, coeffs, sems):
    del after_ref
    parts = coeffs.shape[0]
    whole_sky = pltpu.make_async_copy(sky_ref, sky, sems.at[parts])
    copies = [
        pltpu.make_async_copy(coeffs_ref.at[:, pl.ds(at * width, width)], coeffs.at[at], sems.at[at])
        for at in range(parts)
    ]
    copies[0].start()
    whole_sky.start()
    for copy in copies[1:]:
        copy.start()
    last_ref[...] = jnp.zeros_like(last_ref)
    whole_sky.wait()
    for at in range(parts):
        copies[at].wait()
        direct = jnp.dot(sky[...], coeffs[at], preferred_element_type=jnp.float32)
        if len(out_ref.shape) == 2:
            out_ref[:, at * width : (at + 1) * width] = direct
            continue
        emitted = (albedo_ref[:, at * width : (at + 1) * width] * direct).astype(jnp.bfloat16)
        block = out_ref.shape[2]
        for k in range(width // block):
            out_ref[at * (width // block) + k] = emitted[:, k * block : (k + 1) * block]


def product(after, sky, coeffs, albedo, out, width, name):
    parts = coeffs.shape[1] // width
    return pl.pallas_call(
        functools.partial(product_kernel, width),
        in_specs=[ANY, HBM, HBM, VMEM],
        out_specs=[VMEM, VMEM],
        out_shape=[out, jax.ShapeDtypeStruct((1, 128), jnp.int32)],
        scratch_shapes=[
            pltpu.VMEM(sky.shape, sky.dtype),
            pltpu.VMEM((parts, coeffs.shape[0], width), coeffs.dtype),
            pltpu.SemaphoreType.DMA((parts + 1,)),
        ],
        compiler_params=pltpu.CompilerParams(vmem_limit_bytes=62 * 2**20),
        name=name,
    )(after, sky, coeffs, albedo)


def reads_kernel(blocks, groups, cols_ref, reads_ref):
    slots, width = cols_ref.shape[1], reads_ref.shape[1]
    group = lax.broadcasted_iota(jnp.int32, (groups, slots), 0)
    inside = jnp.broadcast_to(cols_ref[...], (groups, slots)) - group * blocks
    read = (inside >= 0) & (inside < blocks)
    lo = jnp.min(jnp.where(read, inside, blocks - 1), axis=1, keepdims=True)
    hi = jnp.max(jnp.where(read, inside, 0), axis=1, keepdims=True)
    group = lax.broadcasted_iota(jnp.int32, (groups, width), 0)
    lane = lax.broadcasted_iota(jnp.int32, (groups, width), 1)
    row = jnp.where(lane == group, lo, 0) + jnp.where(lane == group + groups, hi, 0)
    live = jnp.sum((cols_ref[...] >= 0).astype(jnp.int32), axis=1, keepdims=True)
    reads_ref[...] = jnp.sum(row, axis=0, keepdims=True) + jnp.where(lane[0:1] == 2 * groups, live, 0)


def blocks_read(cols, blocks, groups):
    width = -(-(2 * groups + 1) // 128) * 128
    return pl.pallas_call(
        functools.partial(reads_kernel, blocks, groups),
        in_specs=[VMEM],
        out_specs=VMEM,
        out_shape=jax.ShapeDtypeStruct((1, width), jnp.int32),
        compiler_params=pltpu.CompilerParams(vmem_limit_bytes=2**20),
        name="reads",
    )(cols.reshape(1, -1))


def pack_kernel(wanted, groups, me_ref, table_ref, *refs):
    held, outs = refs[: -len(wanted)], refs[-len(wanted) :]
    for out, (peer, sends) in zip(outs, wanted):
        for at, (which, bits, end) in enumerate(sends):
            out[at] = held[which][table_ref[peer, (me_ref[0] ^ bits) + groups * end]]


def pack(me, table, groups, held, wanted):
    return pl.pallas_call(
        functools.partial(pack_kernel, wanted, groups),
        in_specs=[SMEM, SMEM] + [VMEM] * len(held),
        out_specs=[VMEM] * len(wanted),
        out_shape=[pltpu.VMEM((len(sends),) + held[0].shape[1:], held[0].dtype) for _, sends in wanted],
        compiler_params=pltpu.CompilerParams(vmem_limit_bytes=24 * 2**20),
        name="pack",
    )(me, table, *held)


def plan_kernel(blocks, rooms, groups, me_ref, rows_ref, cols_ref, reads_ref, phase_ref, base_ref, local_ref, *refs):
    order_ref = refs[-1]
    phases, places = order_ref.shape

    def clear(i, carry):
        for at in range(phases):
            order_ref[at, i] = rooms[at] * 4096
        return carry

    lax.fori_loop(1, places, clear, 0)
    for at in range(phases):
        order_ref[at, 0] = 0

    def step(slot, carry):
        col = cols_ref[slot]
        group = col // blocks
        kind = group ^ me_ref[0]
        inside = col - group * blocks
        local = local_ref[kind] == 1
        end = (inside == reads_ref[0, groups + group]).astype(jnp.int32)
        source = base_ref[kind] + jnp.where(local, inside, end)
        row = rows_ref[slot] - me_ref[0] * blocks
        phase = phase_ref[kind]
        at = order_ref[phase, 0] + 1
        order_ref[phase, at] = slot + row * 256 + source * 4096
        order_ref[phase, 0] = at
        return carry

    lax.fori_loop(0, reads_ref[0, 2 * groups], step, 0)


def plan(me, rows, cols, reads, phase, base, local, after, blocks, rooms):
    return pl.pallas_call(
        functools.partial(plan_kernel, blocks, rooms, phase.shape[0]),
        in_specs=[SMEM] * 7 + [ANY] * len(after),
        out_specs=SMEM,
        out_shape=jax.ShapeDtypeStruct((len(rooms), 1 + rows.shape[0] + AT_ONCE), jnp.int32),
        compiler_params=pltpu.CompilerParams(vmem_limit_bytes=2**20),
        name="plan",
    )(me, rows, cols, reads, phase, base, local, *after)


def reflect_kernel(phase, order_ref, total_ref, views_ref, *refs):
    sources, (out_ref, pool, order, sems) = refs[:-4], refs[-4:]
    copies = [
        pltpu.make_async_copy(total_ref, out_ref, sems.at[len(sources)]),
        pltpu.make_async_copy(order_ref, order, sems.at[len(sources) + 1]),
    ]
    room = 0
    for number, source in enumerate(sources):
        length = source.shape[0]
        copies.append(pltpu.make_async_copy(source, pool.at[pl.ds(room, length)], sems.at[number]))
        room += length
    for copy in copies:
        copy.start()
    pool[room] = jnp.zeros(pool.shape[1:], pool.dtype)
    for copy in copies:
        copy.wait()
    block = views_ref.shape[1]

    def step(i, carry):
        entries = [order[phase, 1 + i * AT_ONCE + k] for k in range(AT_ONCE)]
        parts = [
            lax.dot_general(
                pool[entry // 4096],
                views_ref[entry & 255],
                (((1,), (1,)), ((), ())),
                preferred_element_type=jnp.float32,
            )
            for entry in entries
        ]
        for entry, part in zip(entries, parts):
            columns = pl.ds(pl.multiple_of(((entry // 256) & 15) * block, block), block)
            out_ref[:, columns] += part
        return carry

    lax.fori_loop(0, (order[phase, 0] + AT_ONCE - 1) // AT_ONCE, step, 0)


def reflect(phase, order, total, view_blocks, sources):
    room = sum(source.shape[0] for source in sources)
    return pl.pallas_call(
        functools.partial(reflect_kernel, phase),
        in_specs=[HBM, HBM if phase == 0 else ANY, VMEM] + [ANY] * len(sources),
        out_specs=VMEM,
        out_shape=jax.ShapeDtypeStruct(total.shape, total.dtype),
        scratch_shapes=[
            pltpu.VMEM((room + 1,) + sources[0].shape[1:], sources[0].dtype),
            pltpu.SMEM(order.shape, order.dtype),
            pltpu.SemaphoreType.DMA((len(sources) + 2,)),
        ],
        compiler_params=pltpu.CompilerParams(vmem_limit_bytes=24 * 2**20),
        name="reflect",
    )(order, total, view_blocks, *sources)


def per_device(sky, coeffs, albedo, view_blocks, block_rows, block_cols, counts):
    peers = lax.axis_size("tiles")
    me = lax.axis_index("tiles").astype(jnp.int32).reshape(1)
    block = view_blocks.shape[1]
    blocks = coeffs.shape[1] // block
    rest = peers // NEAR - 1
    far = [NEAR * k for k in range(1, rest + 1)]
    core, beside, below = 1, 2, 4

    def swap(x, bits):
        return lax.ppermute(x, "tiles", [(i, i ^ bits) for i in range(peers)])

    hours, tiles = sky.shape[0], coeffs.shape[1]
    albedo = albedo.reshape(1, -1)
    emitted, zeros = product(
        me, sky, coeffs, albedo, pltpu.VMEM((blocks, hours, block), jnp.bfloat16), 4 * block, "emitted"
    )

    far_held = [swap(emitted, bits) for bits in far]
    below_held = swap(emitted, below)
    beside_held = swap(emitted, beside)

    live = jnp.arange(block_cols.shape[0], dtype=jnp.int32) < counts[0] + zeros[0, 0]
    reads = blocks_read(jnp.where(live, block_cols, -1), blocks, peers)
    table = jnp.concatenate([reads, swap(reads, beside)])
    below_table = swap(table, below)
    direct, zeros = product(
        reads, sky, coeffs, albedo, jax.ShapeDtypeStruct((hours, tiles), jnp.float32), 4 * block, "direct"
    )

    place = {kind: (0, blocks * kind) for kind in range(below)}
    place[below] = (1, 2 * blocks * rest)
    place[below + core] = (1, 2 * blocks * rest + blocks)
    place[below + beside + core] = (1, 2 * blocks * (rest + 1) + 4 * rest)
    place[below + beside] = (2, 4 * rest)
    local = {*range(below), below, below + core}
    for h, bits in enumerate(far):
        for c in range(2):
            local.add(bits + c)
            place[bits + c] = (1, blocks * (2 * h + c))
            place[bits + beside + c] = (1, 2 * blocks * (rest + 1) + 4 * h + 2 * c)
            place[bits + below + c] = (2, 4 * h + 2 * c)
            place[bits + below + beside + c] = (2, 4 * rest + 2 + 4 * h + 2 * c)
    rooms = [4 * blocks, 2 * blocks * (rest + 1) + 4 * rest + 2, 8 * rest + 2]
    order = plan(
        me,
        block_rows,
        block_cols,
        reads,
        jnp.array([place[kind][0] for kind in range(peers)], jnp.int32),
        jnp.array([place[kind][1] for kind in range(peers)], jnp.int32),
        jnp.array([int(kind in local) for kind in range(peers)], jnp.int32),
        [zeros],
        blocks,
        rooms,
    )
    order, below_table, below_held, far_held = lax.optimization_barrier((order, below_table, below_held, far_held))
    table = jnp.concatenate([table, below_table])
    held = [x for shard in far_held for x in (shard, swap(shard, core))]
    below_pair = [below_held, swap(below_held, core)]
    near = [emitted, swap(emitted, core), beside_held, swap(beside_held, core)]

    wanted = [(2 * h + c, far[h] + c, end) for h in range(rest) for c in range(2) for end in range(2)]
    from_beside = [(2 * rest, below + core, end) for end in range(2)]
    from_below = [(2 * rest + 1, beside, end) for end in range(2)]
    sends = [(1, wanted + from_beside), (2, wanted + from_below), (3, wanted)]
    others = pack(me, table, peers, held + [below_pair[1], beside_held], sends)
    late = [swap(x, bits) for x, bits in zip(others, (beside, below, below + beside))]

    direct, _ = lax.optimization_barrier((direct, others[0]))
    total = reflect(0, order, direct, view_blocks, near)
    total = reflect(1, order, total, view_blocks, held + below_pair + late[:1])
    return reflect(2, order, total, view_blocks, late[1:])


def solution(mesh):
    in_specs = (
        P("district", None),
        P(None, ("district", "tiles")),
        P(("district", "tiles")),
        P(("district", "tiles"), None, None),
        P(("district", "tiles")),
        P(("district", "tiles")),
        P(("district", "tiles")),
    )
    out_specs = P(None, ("district", "tiles"))
    return jax.shard_map(
        per_device, mesh=mesh, in_specs=in_specs, out_specs=out_specs, check_vma=False
    )
```

```python
import functools

import jax
import jax.numpy as jnp
from jax import lax
from jax.experimental import pallas as pl
from jax.experimental.pallas import tpu as pltpu
from jax.sharding import PartitionSpec as P

NEAR = 8
AT_ONCE = 8
SMEM = pl.BlockSpec(memory_space=pltpu.SMEM)
VMEM = pl.BlockSpec(memory_space=pltpu.VMEM)
ANY = pl.BlockSpec(memory_space=pl.ANY)
HBM = pl.BlockSpec(memory_space=pltpu.HBM)


def product_kernel(width, after_ref, sky_ref, coeffs_ref, albedo_ref, out_ref, last_ref, sky, coeffs, sems):
    del after_ref
    parts = coeffs.shape[0]
    whole_sky = pltpu.make_async_copy(sky_ref, sky, sems.at[parts])
    copies = [
        pltpu.make_async_copy(coeffs_ref.at[:, pl.ds(at * width, width)], coeffs.at[at], sems.at[at])
        for at in range(parts)
    ]
    copies[0].start()
    whole_sky.start()
    for copy in copies[1:]:
        copy.start()
    last_ref[...] = jnp.zeros_like(last_ref)
    whole_sky.wait()
    for at in range(parts):
        copies[at].wait()
        direct = jnp.dot(sky[...], coeffs[at], preferred_element_type=jnp.float32)
        if len(out_ref.shape) == 2:
            out_ref[:, at * width : (at + 1) * width] = direct
            continue
        emitted = (albedo_ref[:, at * width : (at + 1) * width] * direct).astype(jnp.bfloat16)
        block = out_ref.shape[2]
        for k in range(width // block):
            out_ref[at * (width // block) + k] = emitted[:, k * block : (k + 1) * block]


def product(after, sky, coeffs, albedo, out, width, name):
    parts = coeffs.shape[1] // width
    return pl.pallas_call(
        functools.partial(product_kernel, width),
        in_specs=[ANY, HBM, HBM, VMEM],
        out_specs=[VMEM, VMEM],
        out_shape=[out, jax.ShapeDtypeStruct((1, 128), jnp.int32)],
        scratch_shapes=[
            pltpu.VMEM(sky.shape, sky.dtype),
            pltpu.VMEM((parts, coeffs.shape[0], width), coeffs.dtype),
            pltpu.SemaphoreType.DMA((parts + 1,)),
        ],
        compiler_params=pltpu.CompilerParams(vmem_limit_bytes=62 * 2**20),
        name=name,
    )(after, sky, coeffs, albedo)


def reads_kernel(blocks, groups, cols_ref, reads_ref):
    slots, width = cols_ref.shape[1], reads_ref.shape[1]
    group = lax.broadcasted_iota(jnp.int32, (groups, slots), 0)
    inside = jnp.broadcast_to(cols_ref[...], (groups, slots)) - group * blocks
    read = (inside >= 0) & (inside < blocks)
    lo = jnp.min(jnp.where(read, inside, blocks - 1), axis=1, keepdims=True)
    hi = jnp.max(jnp.where(read, inside, 0), axis=1, keepdims=True)
    group = lax.broadcasted_iota(jnp.int32, (groups, width), 0)
    lane = lax.broadcasted_iota(jnp.int32, (groups, width), 1)
    row = jnp.where(lane == group, lo, 0) + jnp.where(lane == group + groups, hi, 0)
    live = jnp.sum((cols_ref[...] >= 0).astype(jnp.int32), axis=1, keepdims=True)
    reads_ref[...] = jnp.sum(row, axis=0, keepdims=True) + jnp.where(lane[0:1] == 2 * groups, live, 0)


def blocks_read(cols, blocks, groups):
    width = -(-(2 * groups + 1) // 128) * 128
    return pl.pallas_call(
        functools.partial(reads_kernel, blocks, groups),
        in_specs=[VMEM],
        out_specs=VMEM,
        out_shape=jax.ShapeDtypeStruct((1, width), jnp.int32),
        compiler_params=pltpu.CompilerParams(vmem_limit_bytes=2**20),
        name="reads",
    )(cols.reshape(1, -1))


def pack_kernel(wanted, groups, me_ref, table_ref, *refs):
    held, outs = refs[: -len(wanted)], refs[-len(wanted) :]
    for out, (peer, sends) in zip(outs, wanted):
        for at, (which, bits, end) in enumerate(sends):
            out[at] = held[which][table_ref[peer, (me_ref[0] ^ bits) + groups * end]]


def pack(me, table, groups, held, wanted):
    return pl.pallas_call(
        functools.partial(pack_kernel, wanted, groups),
        in_specs=[SMEM, SMEM] + [VMEM] * len(held),
        out_specs=[VMEM] * len(wanted),
        out_shape=[pltpu.VMEM((len(sends),) + held[0].shape[1:], held[0].dtype) for _, sends in wanted],
        compiler_params=pltpu.CompilerParams(vmem_limit_bytes=24 * 2**20),
        name="pack",
    )(me, table, *held)


def plan_kernel(blocks, rooms, groups, me_ref, rows_ref, cols_ref, reads_ref, phase_ref, base_ref, local_ref, *refs):
    order_ref = refs[-1]
    phases, places = order_ref.shape

    def clear(i, carry):
        for at in range(phases):
            order_ref[at, i] = rooms[at] * 4096
        return carry

    lax.fori_loop(1, places, clear, 0)
    for at in range(phases):
        order_ref[at, 0] = 0

    def step(slot, carry):
        col = cols_ref[slot]
        group = col // blocks
        kind = group ^ me_ref[0]
        inside = col - group * blocks
        local = local_ref[kind] == 1
        end = (inside == reads_ref[0, groups + group]).astype(jnp.int32)
        source = base_ref[kind] + jnp.where(local, inside, end)
        row = rows_ref[slot] - me_ref[0] * blocks
        phase = phase_ref[kind]
        at = order_ref[phase, 0] + 1
        order_ref[phase, at] = slot + row * 256 + source * 4096
        order_ref[phase, 0] = at
        return carry

    lax.fori_loop(0, reads_ref[0, 2 * groups], step, 0)


def plan(me, rows, cols, reads, phase, base, local, after, blocks, rooms):
    return pl.pallas_call(
        functools.partial(plan_kernel, blocks, rooms, phase.shape[0]),
        in_specs=[SMEM] * 7 + [ANY] * len(after),
        out_specs=SMEM,
        out_shape=jax.ShapeDtypeStruct((len(rooms), 1 + rows.shape[0] + AT_ONCE), jnp.int32),
        compiler_params=pltpu.CompilerParams(vmem_limit_bytes=2**20),
        name="plan",
    )(me, rows, cols, reads, phase, base, local, *after)


def reflect_kernel(phase, order_ref, total_ref, views_ref, *refs):
    sources, (out_ref, pool, order, sems) = refs[:-4], refs[-4:]
    copies = [pltpu.make_async_copy(order_ref, order, sems.at[len(sources) + 1])]
    if phase == 0:
        copies.append(pltpu.make_async_copy(total_ref, out_ref, sems.at[len(sources)]))
    room = 0
    for number, source in enumerate(sources):
        length = source.shape[0]
        if phase < 2:
            copies.append(pltpu.make_async_copy(source, pool.at[pl.ds(room, length)], sems.at[number]))
        else:
            pool[room : room + length] = source[...]
        room += length
    for copy in copies:
        copy.start()
    pool[room] = jnp.zeros(pool.shape[1:], pool.dtype)
    if phase:
        out_ref[...] = total_ref[...]
    for copy in copies:
        copy.wait()
    block = views_ref.shape[1]

    def step(i, carry):
        entries = [order[phase, 1 + i * AT_ONCE + k] for k in range(AT_ONCE)]
        parts = [
            lax.dot_general(
                pool[entry // 4096],
                views_ref[entry & 255],
                (((1,), (1,)), ((), ())),
                preferred_element_type=jnp.float32,
            )
            for entry in entries
        ]
        for entry, part in zip(entries, parts):
            columns = pl.ds(pl.multiple_of(((entry // 256) & 15) * block, block), block)
            out_ref[:, columns] += part
        return carry

    lax.fori_loop(0, (order[phase, 0] + AT_ONCE - 1) // AT_ONCE, step, 0)


def reflect(phase, order, total, view_blocks, sources):
    room = sum(source.shape[0] for source in sources)
    return pl.pallas_call(
        functools.partial(reflect_kernel, phase),
        in_specs=[HBM, HBM if phase == 0 else VMEM, VMEM] + [ANY if phase < 2 else VMEM] * len(sources),
        out_specs=VMEM,
        out_shape=jax.ShapeDtypeStruct(total.shape, total.dtype),
        scratch_shapes=[
            pltpu.VMEM((room + 1,) + sources[0].shape[1:], sources[0].dtype),
            pltpu.SMEM(order.shape, order.dtype),
            pltpu.SemaphoreType.DMA((len(sources) + 2,)),
        ],
        compiler_params=pltpu.CompilerParams(vmem_limit_bytes=24 * 2**20),
        name="reflect",
    )(order, total, view_blocks, *sources)


def per_device(sky, coeffs, albedo, view_blocks, block_rows, block_cols, counts):
    peers = lax.axis_size("tiles")
    me = lax.axis_index("tiles").astype(jnp.int32).reshape(1)
    block = view_blocks.shape[1]
    blocks = coeffs.shape[1] // block
    rest = peers // NEAR - 1
    far = [NEAR * k for k in range(1, rest + 1)]
    core, beside, below = 1, 2, 4

    def swap(x, bits):
        return lax.ppermute(x, "tiles", [(i, i ^ bits) for i in range(peers)])

    hours, tiles = sky.shape[0], coeffs.shape[1]
    albedo = albedo.reshape(1, -1)
    emitted, zeros = product(
        me, sky, coeffs, albedo, pltpu.VMEM((blocks, hours, block), jnp.bfloat16), 4 * block, "emitted"
    )

    far_held = [swap(emitted, bits) for bits in far]
    below_held = swap(emitted, below)
    beside_held = swap(emitted, beside)

    live = jnp.arange(block_cols.shape[0], dtype=jnp.int32) < counts[0] + zeros[0, 0]
    reads = blocks_read(jnp.where(live, block_cols, -1), blocks, peers)
    table = jnp.concatenate([reads, swap(reads, beside)])
    below_table = swap(table, below)
    direct, zeros = product(
        reads, sky, coeffs, albedo, jax.ShapeDtypeStruct((hours, tiles), jnp.float32), 4 * block, "direct"
    )

    place = {kind: (0, blocks * kind) for kind in range(below)}
    place[below] = (1, 2 * blocks * rest)
    place[below + core] = (1, 2 * blocks * rest + blocks)
    place[below + beside + core] = (1, 2 * blocks * (rest + 1) + 4 * rest)
    place[below + beside] = (2, 4 * rest)
    local = {*range(below), below, below + core}
    for h, bits in enumerate(far):
        for c in range(2):
            local.add(bits + c)
            place[bits + c] = (1, blocks * (2 * h + c))
            place[bits + beside + c] = (1, 2 * blocks * (rest + 1) + 4 * h + 2 * c)
            place[bits + below + c] = (2, 4 * h + 2 * c)
            place[bits + below + beside + c] = (2, 4 * rest + 2 + 4 * h + 2 * c)
    rooms = [4 * blocks, 2 * blocks * (rest + 1) + 4 * rest + 2, 8 * rest + 2]
    order = plan(
        me,
        block_rows,
        block_cols,
        reads,
        jnp.array([place[kind][0] for kind in range(peers)], jnp.int32),
        jnp.array([place[kind][1] for kind in range(peers)], jnp.int32),
        jnp.array([int(kind in local) for kind in range(peers)], jnp.int32),
        [zeros],
        blocks,
        rooms,
    )
    order, below_table, below_held, far_held = lax.optimization_barrier((order, below_table, below_held, far_held))
    table = jnp.concatenate([table, below_table])
    held = [x for shard in far_held for x in (shard, swap(shard, core))]
    below_pair = [below_held, swap(below_held, core)]
    near = [emitted, swap(emitted, core), beside_held, swap(beside_held, core)]

    wanted = [(2 * h + c, far[h] + c, end) for h in range(rest) for c in range(2) for end in range(2)]
    from_beside = [(2 * rest, below + core, end) for end in range(2)]
    from_below = [(2 * rest + 1, beside, end) for end in range(2)]
    sends = [(1, wanted + from_beside), (2, wanted + from_below), (3, wanted)]
    others = pack(me, table, peers, held + [below_pair[1], beside_held], sends)
    late = [swap(x, bits) for x, bits in zip(others, (beside, below, below + beside))]

    direct, _ = lax.optimization_barrier((direct, others[0]))
    total = reflect(0, order, direct, view_blocks, near)
    total = reflect(1, order, total, view_blocks, held + below_pair + late[:1])
    return reflect(2, order, total, view_blocks, late[1:])


def solution(mesh):
    in_specs = (
        P("district", None),
        P(None, ("district", "tiles")),
        P(("district", "tiles")),
        P(("district", "tiles"), None, None),
        P(("district", "tiles")),
        P(("district", "tiles")),
        P(("district", "tiles")),
    )
    out_specs = P(None, ("district", "tiles"))
    return jax.shard_map(
        per_device, mesh=mesh, in_specs=in_specs, out_specs=out_specs, check_vma=False
    )
```

```python
import functools

import jax
import jax.numpy as jnp
from jax import lax
from jax.experimental import pallas as pl
from jax.experimental.pallas import tpu as pltpu
from jax.sharding import PartitionSpec as P

NEAR = 8
AT_ONCE = 8
SMEM = pl.BlockSpec(memory_space=pltpu.SMEM)
VMEM = pl.BlockSpec(memory_space=pltpu.VMEM)
ANY = pl.BlockSpec(memory_space=pl.ANY)
HBM = pl.BlockSpec(memory_space=pltpu.HBM)


def product_kernel(cuts, after_ref, sky_ref, coeffs_ref, albedo_ref, out_ref, last_ref, sky, *scratch):
    del after_ref
    *coeffs, total, sems = scratch
    whole_sky = pltpu.make_async_copy(sky_ref, sky, sems.at[len(coeffs)])
    copies = [
        pltpu.make_async_copy(coeffs_ref.at[pl.ds(start, stop - start)], part, sems.at[number])
        for number, (start, stop, part) in enumerate(zip(cuts, cuts[1:], coeffs))
    ]
    copies[0].start()
    whole_sky.start()
    for copy in copies[1:]:
        copy.start()
    last_ref[...] = jnp.zeros_like(last_ref)
    whole_sky.wait()
    for copy, start, stop, part in zip(copies, cuts, cuts[1:], coeffs):
        copy.wait()
        direct = jnp.dot(sky[:, start:stop], part[...], preferred_element_type=jnp.float32)
        if start:
            direct += total[...]
        if stop < cuts[-1]:
            total[...] = direct
    if len(out_ref.shape) == 2:
        out_ref[...] = direct
        return
    emitted = (albedo_ref[...] * direct).astype(jnp.bfloat16)
    block = out_ref.shape[2]
    for k in range(out_ref.shape[0]):
        out_ref[k] = emitted[:, k * block : (k + 1) * block]


def product(after, sky, coeffs, albedo, out, depth, name):
    patches, tiles = coeffs.shape
    cuts = [*range(0, patches - depth + 1, depth), patches]
    return pl.pallas_call(
        functools.partial(product_kernel, cuts),
        in_specs=[ANY, HBM, HBM, VMEM],
        out_specs=[VMEM, VMEM],
        out_shape=[out, jax.ShapeDtypeStruct((1, 128), jnp.int32)],
        scratch_shapes=[
            pltpu.VMEM(sky.shape, sky.dtype),
            *[pltpu.VMEM((stop - start, tiles), coeffs.dtype) for start, stop in zip(cuts, cuts[1:])],
            pltpu.VMEM((sky.shape[0], tiles), jnp.float32),
            pltpu.SemaphoreType.DMA((len(cuts),)),
        ],
        compiler_params=pltpu.CompilerParams(vmem_limit_bytes=62 * 2**20),
        name=name,
    )(after, sky, coeffs, albedo)


def reads_kernel(blocks, groups, cols_ref, reads_ref):
    slots, width = cols_ref.shape[1], reads_ref.shape[1]
    group = lax.broadcasted_iota(jnp.int32, (groups, slots), 0)
    inside = jnp.broadcast_to(cols_ref[...], (groups, slots)) - group * blocks
    read = (inside >= 0) & (inside < blocks)
    lo = jnp.min(jnp.where(read, inside, blocks - 1), axis=1, keepdims=True)
    hi = jnp.max(jnp.where(read, inside, 0), axis=1, keepdims=True)
    group = lax.broadcasted_iota(jnp.int32, (groups, width), 0)
    lane = lax.broadcasted_iota(jnp.int32, (groups, width), 1)
    row = jnp.where(lane == group, lo, 0) + jnp.where(lane == group + groups, hi, 0)
    live = jnp.sum((cols_ref[...] >= 0).astype(jnp.int32), axis=1, keepdims=True)
    reads_ref[...] = jnp.sum(row, axis=0, keepdims=True) + jnp.where(lane[0:1] == 2 * groups, live, 0)


def blocks_read(cols, blocks, groups):
    width = -(-(2 * groups + 1) // 128) * 128
    return pl.pallas_call(
        functools.partial(reads_kernel, blocks, groups),
        in_specs=[VMEM],
        out_specs=VMEM,
        out_shape=jax.ShapeDtypeStruct((1, width), jnp.int32),
        compiler_params=pltpu.CompilerParams(vmem_limit_bytes=2**20),
        name="reads",
    )(cols.reshape(1, -1))


def pack_kernel(wanted, groups, me_ref, table_ref, *refs):
    held, outs = refs[: -len(wanted)], refs[-len(wanted) :]
    for out, (peer, sends) in zip(outs, wanted):
        for at, (which, bits, end) in enumerate(sends):
            out[at] = held[which][table_ref[peer, (me_ref[0] ^ bits) + groups * end]]


def pack(me, table, groups, held, wanted):
    return pl.pallas_call(
        functools.partial(pack_kernel, wanted, groups),
        in_specs=[SMEM, SMEM] + [VMEM] * len(held),
        out_specs=[VMEM] * len(wanted),
        out_shape=[pltpu.VMEM((len(sends),) + held[0].shape[1:], held[0].dtype) for _, sends in wanted],
        compiler_params=pltpu.CompilerParams(vmem_limit_bytes=24 * 2**20),
        name="pack",
    )(me, table, *held)


def plan_kernel(blocks, rooms, groups, me_ref, rows_ref, cols_ref, reads_ref, phase_ref, base_ref, local_ref, *refs):
    order_ref = refs[-1]
    phases, places = order_ref.shape

    def clear(i, carry):
        for at in range(phases):
            order_ref[at, i] = rooms[at] * 4096
        return carry

    lax.fori_loop(1, places, clear, 0)
    for at in range(phases):
        order_ref[at, 0] = 0

    def step(slot, carry):
        col = cols_ref[slot]
        group = col // blocks
        kind = group ^ me_ref[0]
        inside = col - group * blocks
        local = local_ref[kind] == 1
        end = (inside == reads_ref[0, groups + group]).astype(jnp.int32)
        source = base_ref[kind] + jnp.where(local, inside, end)
        row = rows_ref[slot] - me_ref[0] * blocks
        phase = phase_ref[kind]
        at = order_ref[phase, 0] + 1
        order_ref[phase, at] = slot + row * 256 + source * 4096
        order_ref[phase, 0] = at
        return carry

    lax.fori_loop(0, reads_ref[0, 2 * groups], step, 0)


def plan(me, rows, cols, reads, phase, base, local, after, blocks, rooms):
    return pl.pallas_call(
        functools.partial(plan_kernel, blocks, rooms, phase.shape[0]),
        in_specs=[SMEM] * 7 + [ANY] * len(after),
        out_specs=SMEM,
        out_shape=jax.ShapeDtypeStruct((len(rooms), 1 + rows.shape[0] + AT_ONCE), jnp.int32),
        compiler_params=pltpu.CompilerParams(vmem_limit_bytes=2**20),
        name="plan",
    )(me, rows, cols, reads, phase, base, local, *after)


def reflect_kernel(phase, order_ref, total_ref, views_ref, *refs):
    sources, (out_ref, pool, order, sems) = refs[:-4], refs[-4:]
    copies = [pltpu.make_async_copy(order_ref, order, sems.at[len(sources) + 1])]
    if phase == 0:
        copies.append(pltpu.make_async_copy(total_ref, out_ref, sems.at[len(sources)]))
    room = 0
    for number, source in enumerate(sources):
        length = source.shape[0]
        if phase < 2:
            copies.append(pltpu.make_async_copy(source, pool.at[pl.ds(room, length)], sems.at[number]))
        else:
            pool[room : room + length] = source[...]
        room += length
    for copy in copies:
        copy.start()
    pool[room] = jnp.zeros(pool.shape[1:], pool.dtype)
    if phase:
        out_ref[...] = total_ref[...]
    for copy in copies:
        copy.wait()
    block = views_ref.shape[1]

    def step(i, carry):
        entries = [order[phase, 1 + i * AT_ONCE + k] for k in range(AT_ONCE)]
        parts = [
            lax.dot_general(
                pool[entry // 4096],
                views_ref[entry & 255],
                (((1,), (1,)), ((), ())),
                preferred_element_type=jnp.float32,
            )
            for entry in entries
        ]
        for entry, part in zip(entries, parts):
            columns = pl.ds(pl.multiple_of(((entry // 256) & 15) * block, block), block)
            out_ref[:, columns] += part
        return carry

    lax.fori_loop(0, (order[phase, 0] + AT_ONCE - 1) // AT_ONCE, step, 0)


def reflect(phase, order, total, view_blocks, sources):
    room = sum(source.shape[0] for source in sources)
    return pl.pallas_call(
        functools.partial(reflect_kernel, phase),
        in_specs=[HBM, HBM if phase == 0 else VMEM, VMEM] + [ANY if phase < 2 else VMEM] * len(sources),
        out_specs=VMEM,
        out_shape=jax.ShapeDtypeStruct(total.shape, total.dtype),
        scratch_shapes=[
            pltpu.VMEM((room + 1,) + sources[0].shape[1:], sources[0].dtype),
            pltpu.SMEM(order.shape, order.dtype),
            pltpu.SemaphoreType.DMA((len(sources) + 2,)),
        ],
        compiler_params=pltpu.CompilerParams(vmem_limit_bytes=24 * 2**20),
        name="reflect",
    )(order, total, view_blocks, *sources)


def per_device(sky, coeffs, albedo, view_blocks, block_rows, block_cols, counts):
    peers = lax.axis_size("tiles")
    me = lax.axis_index("tiles").astype(jnp.int32).reshape(1)
    block = view_blocks.shape[1]
    blocks = coeffs.shape[1] // block
    rest = peers // NEAR - 1
    far = [NEAR * k for k in range(1, rest + 1)]
    core, beside, below = 1, 2, 4

    def swap(x, bits):
        return lax.ppermute(x, "tiles", [(i, i ^ bits) for i in range(peers)])

    hours, tiles = sky.shape[0], coeffs.shape[1]
    albedo = albedo.reshape(1, -1)
    emitted, zeros = product(
        me, sky, coeffs, albedo, pltpu.VMEM((blocks, hours, block), jnp.bfloat16), 2 * block, "emitted"
    )

    far_held = [swap(emitted, bits) for bits in far]
    below_held = swap(emitted, below)
    beside_held = swap(emitted, beside)

    live = jnp.arange(block_cols.shape[0], dtype=jnp.int32) < counts[0] + zeros[0, 0]
    reads = blocks_read(jnp.where(live, block_cols, -1), blocks, peers)
    table = jnp.concatenate([reads, swap(reads, beside)])
    below_table = swap(table, below)
    direct, zeros = product(
        reads, sky, coeffs, albedo, jax.ShapeDtypeStruct((hours, tiles), jnp.float32), 2 * block, "direct"
    )

    place = {kind: (0, blocks * kind) for kind in range(below)}
    place[below] = (1, 2 * blocks * rest)
    place[below + core] = (1, 2 * blocks * rest + blocks)
    place[below + beside + core] = (1, 2 * blocks * (rest + 1) + 4 * rest)
    place[below + beside] = (2, 4 * rest)
    local = {*range(below), below, below + core}
    for h, bits in enumerate(far):
        for c in range(2):
            local.add(bits + c)
            place[bits + c] = (1, blocks * (2 * h + c))
            place[bits + beside + c] = (1, 2 * blocks * (rest + 1) + 4 * h + 2 * c)
            place[bits + below + c] = (2, 4 * h + 2 * c)
            place[bits + below + beside + c] = (2, 4 * rest + 2 + 4 * h + 2 * c)
    rooms = [4 * blocks, 2 * blocks * (rest + 1) + 4 * rest + 2, 8 * rest + 2]
    order = plan(
        me,
        block_rows,
        block_cols,
        reads,
        jnp.array([place[kind][0] for kind in range(peers)], jnp.int32),
        jnp.array([place[kind][1] for kind in range(peers)], jnp.int32),
        jnp.array([int(kind in local) for kind in range(peers)], jnp.int32),
        [zeros],
        blocks,
        rooms,
    )
    order, below_table, below_held, far_held = lax.optimization_barrier((order, below_table, below_held, far_held))
    table = jnp.concatenate([table, below_table])
    held = [x for shard in far_held for x in (shard, swap(shard, core))]
    below_pair = [below_held, swap(below_held, core)]
    near = [emitted, swap(emitted, core), beside_held, swap(beside_held, core)]

    wanted = [(2 * h + c, far[h] + c, end) for h in range(rest) for c in range(2) for end in range(2)]
    from_beside = [(2 * rest, below + core, end) for end in range(2)]
    from_below = [(2 * rest + 1, beside, end) for end in range(2)]
    sends = [(1, wanted + from_beside), (2, wanted + from_below), (3, wanted)]
    others = pack(me, table, peers, held + [below_pair[1], beside_held], sends)
    late = [swap(x, bits) for x, bits in zip(others, (beside, below, below + beside))]

    direct, _ = lax.optimization_barrier((direct, others[0]))
    total = reflect(0, order, direct, view_blocks, near)
    total = reflect(1, order, total, view_blocks, held + below_pair + late[:1])
    return reflect(2, order, total, view_blocks, late[1:])


def solution(mesh):
    in_specs = (
        P("district", None),
        P(None, ("district", "tiles")),
        P(("district", "tiles")),
        P(("district", "tiles"), None, None),
        P(("district", "tiles")),
        P(("district", "tiles")),
        P(("district", "tiles")),
    )
    out_specs = P(None, ("district", "tiles"))
    return jax.shard_map(
        per_device, mesh=mesh, in_specs=in_specs, out_specs=out_specs, check_vma=False
    )
```

```python
import functools

import jax
import jax.numpy as jnp
from jax import lax
from jax.experimental import pallas as pl
from jax.experimental.pallas import tpu as pltpu
from jax.sharding import PartitionSpec as P

NEAR = 8
AT_ONCE = 8
SMEM = pl.BlockSpec(memory_space=pltpu.SMEM)
VMEM = pl.BlockSpec(memory_space=pltpu.VMEM)
ANY = pl.BlockSpec(memory_space=pl.ANY)
HBM = pl.BlockSpec(memory_space=pltpu.HBM)


def product_kernel(cuts, after_ref, sky_ref, coeffs_ref, albedo_ref, out_ref, last_ref, sky, *scratch):
    del after_ref
    *coeffs, total, sems = scratch
    whole_sky = pltpu.make_async_copy(sky_ref, sky, sems.at[len(coeffs)])
    copies = [
        pltpu.make_async_copy(coeffs_ref.at[pl.ds(start, stop - start)], part, sems.at[number])
        for number, (start, stop, part) in enumerate(zip(cuts, cuts[1:], coeffs))
    ]
    copies[0].start()
    whole_sky.start()
    for copy in copies[1:]:
        copy.start()
    last_ref[...] = jnp.zeros_like(last_ref)
    whole_sky.wait()
    for copy, start, stop, part in zip(copies, cuts, cuts[1:], coeffs):
        copy.wait()
        direct = jnp.dot(sky[:, start:stop], part[...], preferred_element_type=jnp.float32)
        if start:
            direct += total[...]
        if stop < cuts[-1]:
            total[...] = direct
    if len(out_ref.shape) == 2:
        out_ref[...] = direct
        return
    emitted = (albedo_ref[...] * direct).astype(jnp.bfloat16)
    block = out_ref.shape[2]
    for k in range(out_ref.shape[0]):
        out_ref[k] = emitted[:, k * block : (k + 1) * block]


def product(after, sky, coeffs, albedo, out, depth, name):
    patches, tiles = coeffs.shape
    cuts = [*range(0, patches - depth + 1, depth), patches]
    return pl.pallas_call(
        functools.partial(product_kernel, cuts),
        in_specs=[ANY, HBM, HBM, VMEM],
        out_specs=[VMEM, VMEM],
        out_shape=[out, jax.ShapeDtypeStruct((1, 128), jnp.int32)],
        scratch_shapes=[
            pltpu.VMEM(sky.shape, sky.dtype),
            *[pltpu.VMEM((stop - start, tiles), coeffs.dtype) for start, stop in zip(cuts, cuts[1:])],
            pltpu.VMEM((sky.shape[0], tiles), jnp.float32),
            pltpu.SemaphoreType.DMA((len(cuts),)),
        ],
        compiler_params=pltpu.CompilerParams(vmem_limit_bytes=62 * 2**20),
        name=name,
    )(after, sky, coeffs, albedo)


def reads_kernel(blocks, groups, cols_ref, reads_ref):
    slots, width = cols_ref.shape[1], reads_ref.shape[1]
    group = lax.broadcasted_iota(jnp.int32, (groups, slots), 0)
    inside = jnp.broadcast_to(cols_ref[...], (groups, slots)) - group * blocks
    read = (inside >= 0) & (inside < blocks)
    lo = jnp.min(jnp.where(read, inside, blocks - 1), axis=1, keepdims=True)
    hi = jnp.max(jnp.where(read, inside, 0), axis=1, keepdims=True)
    group = lax.broadcasted_iota(jnp.int32, (groups, width), 0)
    lane = lax.broadcasted_iota(jnp.int32, (groups, width), 1)
    row = jnp.where(lane == group, lo, 0) + jnp.where(lane == group + groups, hi, 0)
    live = jnp.sum((cols_ref[...] >= 0).astype(jnp.int32), axis=1, keepdims=True)
    reads_ref[...] = jnp.sum(row, axis=0, keepdims=True) + jnp.where(lane[0:1] == 2 * groups, live, 0)


def blocks_read(cols, blocks, groups):
    width = -(-(2 * groups + 1) // 128) * 128
    return pl.pallas_call(
        functools.partial(reads_kernel, blocks, groups),
        in_specs=[VMEM],
        out_specs=VMEM,
        out_shape=jax.ShapeDtypeStruct((1, width), jnp.int32),
        compiler_params=pltpu.CompilerParams(vmem_limit_bytes=2**20),
        name="reads",
    )(cols.reshape(1, -1))


def pack_kernel(wanted, groups, me_ref, table_ref, *refs):
    held, outs = refs[: -len(wanted)], refs[-len(wanted) :]
    for out, (peer, sends) in zip(outs, wanted):
        for at, (which, bits, end) in enumerate(sends):
            out[at] = held[which][table_ref[peer, (me_ref[0] ^ bits) + groups * end]]


def pack(me, table, groups, held, wanted):
    return pl.pallas_call(
        functools.partial(pack_kernel, wanted, groups),
        in_specs=[SMEM, SMEM] + [VMEM] * len(held),
        out_specs=[VMEM] * len(wanted),
        out_shape=[pltpu.VMEM((len(sends),) + held[0].shape[1:], held[0].dtype) for _, sends in wanted],
        compiler_params=pltpu.CompilerParams(vmem_limit_bytes=24 * 2**20),
        name="pack",
    )(me, table, *held)


def plan_kernel(blocks, rooms, groups, me_ref, rows_ref, cols_ref, reads_ref, phase_ref, base_ref, local_ref, *refs):
    order_ref = refs[-1]
    phases, places = order_ref.shape

    def clear(i, carry):
        for at in range(phases):
            order_ref[at, i] = rooms[at] * 4096
        return carry

    lax.fori_loop(1, places, clear, 0)
    for at in range(phases):
        order_ref[at, 0] = 0

    def step(slot, carry):
        col = cols_ref[slot]
        group = col >> (blocks.bit_length() - 1)
        kind = group ^ me_ref[0]
        inside = col & (blocks - 1)
        local = local_ref[kind] == 1
        end = (inside == reads_ref[0, groups + group]).astype(jnp.int32)
        source = base_ref[kind] + jnp.where(local, inside, end)
        row = rows_ref[slot] & (blocks - 1)
        phase = phase_ref[kind]
        at = order_ref[phase, 0] + 1
        order_ref[phase, at] = slot | (row << 8) | (source << 12)
        order_ref[phase, 0] = at
        return carry

    lax.fori_loop(0, reads_ref[0, 2 * groups], step, 0)


def plan(me, rows, cols, reads, phase, base, local, after, blocks, rooms):
    return pl.pallas_call(
        functools.partial(plan_kernel, blocks, rooms, phase.shape[0]),
        in_specs=[SMEM] * 7 + [ANY] * len(after),
        out_specs=SMEM,
        out_shape=jax.ShapeDtypeStruct((len(rooms), 1 + rows.shape[0] + AT_ONCE), jnp.int32),
        compiler_params=pltpu.CompilerParams(vmem_limit_bytes=2**20),
        name="plan",
    )(me, rows, cols, reads, phase, base, local, *after)


def reflect_kernel(phase, order_ref, total_ref, views_ref, *refs):
    sources, (out_ref, pool, order, sems) = refs[:-4], refs[-4:]
    copies = [pltpu.make_async_copy(order_ref, order, sems.at[len(sources) + 1])]
    if phase == 0:
        copies.append(pltpu.make_async_copy(total_ref, out_ref, sems.at[len(sources)]))
    room = 0
    for number, source in enumerate(sources):
        length = source.shape[0]
        if phase < 2:
            copies.append(pltpu.make_async_copy(source, pool.at[pl.ds(room, length)], sems.at[number]))
        else:
            pool[room : room + length] = source[...]
        room += length
    for copy in copies:
        copy.start()
    pool[room] = jnp.zeros(pool.shape[1:], pool.dtype)
    if phase:
        out_ref[...] = total_ref[...]
    for copy in copies:
        copy.wait()
    block = views_ref.shape[1]

    def step(i, carry):
        entries = [order[phase, 1 + i * AT_ONCE + k] for k in range(AT_ONCE)]
        parts = [
            lax.dot_general(
                pool[entry >> 12],
                views_ref[entry & 255],
                (((1,), (1,)), ((), ())),
                preferred_element_type=jnp.float32,
            )
            for entry in entries
        ]
        for entry, part in zip(entries, parts):
            columns = pl.ds(pl.multiple_of(((entry >> 8) & 15) * block, block), block)
            out_ref[:, columns] += part
        return carry

    lax.fori_loop(0, (order[phase, 0] + AT_ONCE - 1) // AT_ONCE, step, 0)


def reflect(phase, order, total, view_blocks, sources):
    room = sum(source.shape[0] for source in sources)
    return pl.pallas_call(
        functools.partial(reflect_kernel, phase),
        in_specs=[HBM, HBM if phase == 0 else VMEM, VMEM] + [ANY if phase < 2 else VMEM] * len(sources),
        out_specs=VMEM,
        out_shape=jax.ShapeDtypeStruct(total.shape, total.dtype),
        scratch_shapes=[
            pltpu.VMEM((room + 1,) + sources[0].shape[1:], sources[0].dtype),
            pltpu.SMEM(order.shape, order.dtype),
            pltpu.SemaphoreType.DMA((len(sources) + 2,)),
        ],
        compiler_params=pltpu.CompilerParams(vmem_limit_bytes=24 * 2**20),
        name="reflect",
    )(order, total, view_blocks, *sources)


def per_device(sky, coeffs, albedo, view_blocks, block_rows, block_cols, counts):
    peers = lax.axis_size("tiles")
    me = lax.axis_index("tiles").astype(jnp.int32).reshape(1)
    block = view_blocks.shape[1]
    blocks = coeffs.shape[1] // block
    rest = peers // NEAR - 1
    far = [NEAR * k for k in range(1, rest + 1)]
    core, beside, below = 1, 2, 4

    def swap(x, bits):
        return lax.ppermute(x, "tiles", [(i, i ^ bits) for i in range(peers)])

    hours, tiles = sky.shape[0], coeffs.shape[1]
    albedo = albedo.reshape(1, -1)
    emitted, zeros = product(
        me, sky, coeffs, albedo, pltpu.VMEM((blocks, hours, block), jnp.bfloat16), 2 * block, "emitted"
    )

    far_held = [swap(emitted, bits) for bits in far]
    below_held = swap(emitted, below)
    beside_held = swap(emitted, beside)

    live = jnp.arange(block_cols.shape[0], dtype=jnp.int32) < counts[0] + zeros[0, 0]
    reads = blocks_read(jnp.where(live, block_cols, -1), blocks, peers)
    table = jnp.concatenate([reads, swap(reads, beside)])
    below_table = swap(table, below)
    direct, zeros = product(
        reads, sky, coeffs, albedo, jax.ShapeDtypeStruct((hours, tiles), jnp.float32), 2 * block, "direct"
    )

    place = {kind: (0, blocks * kind) for kind in range(below)}
    place[below] = (1, 2 * blocks * rest)
    place[below + core] = (1, 2 * blocks * rest + blocks)
    place[below + beside + core] = (1, 2 * blocks * (rest + 1) + 4 * rest)
    place[below + beside] = (2, 4 * rest)
    local = {*range(below), below, below + core}
    for h, bits in enumerate(far):
        for c in range(2):
            local.add(bits + c)
            place[bits + c] = (1, blocks * (2 * h + c))
            place[bits + beside + c] = (1, 2 * blocks * (rest + 1) + 4 * h + 2 * c)
            place[bits + below + c] = (2, 4 * h + 2 * c)
            place[bits + below + beside + c] = (2, 4 * rest + 2 + 4 * h + 2 * c)
    rooms = [4 * blocks, 2 * blocks * (rest + 1) + 4 * rest + 2, 8 * rest + 2]
    order = plan(
        me,
        block_rows,
        block_cols,
        reads,
        jnp.array([place[kind][0] for kind in range(peers)], jnp.int32),
        jnp.array([place[kind][1] for kind in range(peers)], jnp.int32),
        jnp.array([int(kind in local) for kind in range(peers)], jnp.int32),
        [zeros],
        blocks,
        rooms,
    )
    order, below_table, below_held, far_held = lax.optimization_barrier((order, below_table, below_held, far_held))
    table = jnp.concatenate([table, below_table])
    held = [x for shard in far_held for x in (shard, swap(shard, core))]
    below_pair = [below_held, swap(below_held, core)]
    near = [emitted, swap(emitted, core), beside_held, swap(beside_held, core)]

    wanted = [(2 * h + c, far[h] + c, end) for h in range(rest) for c in range(2) for end in range(2)]
    from_beside = [(2 * rest, below + core, end) for end in range(2)]
    from_below = [(2 * rest + 1, beside, end) for end in range(2)]
    sends = [(1, wanted + from_beside), (2, wanted + from_below), (3, wanted)]
    others = pack(me, table, peers, held + [below_pair[1], beside_held], sends)
    late = [swap(x, bits) for x, bits in zip(others, (beside, below, below + beside))]

    direct, _ = lax.optimization_barrier((direct, others[0]))
    total = reflect(0, order, direct, view_blocks, near)
    total = reflect(1, order, total, view_blocks, held + below_pair + late[:1])
    return reflect(2, order, total, view_blocks, late[1:])


def solution(mesh):
    in_specs = (
        P("district", None),
        P(None, ("district", "tiles")),
        P(("district", "tiles")),
        P(("district", "tiles"), None, None),
        P(("district", "tiles")),
        P(("district", "tiles")),
        P(("district", "tiles")),
    )
    out_specs = P(None, ("district", "tiles"))
    return jax.shard_map(
        per_device, mesh=mesh, in_specs=in_specs, out_specs=out_specs, check_vma=False
    )
```
